256 devices in a mesh: row: 8 (over x, core), col: 32 (over y, z).
Axes of the slice: x: 4, y: 4, z: 8, core: 2. Of those that a mesh axis runs over, the one named last changes fastest.
Arguments:
- step: int32 [1], replicated, may hold values from 0 to 28
- rhs: float32 [12288, 27648], P('row', 'col'), may hold values from -6 to 6
- panels: float32 [12288, 8192], P('row', 'col'), may hold values from -0.375 to 0.375
- diag_inverses: float32 [256, 8192], P(None, 'col'), may hold values from -2 to 2, as said below
Outputs:
- updated: float32 [12288, 27648], P('row', 'col')
The draws below stay inside these ranges and needn't reach their ends.
Inputs may be any that keep to these rules, and one draw needn't show every extreme that they name: `diag_inverses`: each 256-column block is lower triangular with a positive diagonal.
All inputs are finite; a program needn't handle non-finite values.
Results may differ from the reference program's by a relative error of at most 0.00018.
Values sent between devices are 32-bit elements; how exact they have to be, the bound alone decides.
A program may use at most 128 MiB of HBM per device.

```python
import jax
import jax.numpy as jnp
from jax import lax

NB = 256
K = 27648
BLK_DEV = 6
STEPS = 4
ROWS = 12288
N_ROW = 8
N_COL = 32


def draw_diag_inverses(key, part):
    key = jax.random.fold_in(key, 11)
    key_off, key_diag = jax.random.split(key)
    shape = (NB, NB * N_COL)
    row_index = jnp.arange(NB, dtype=jnp.int32)[:, None]
    col_index = (jnp.arange(NB * N_COL, dtype=jnp.int32) % NB)[None, :]
    off = jnp.clip(jax.random.normal(key_off, shape, jnp.float32), -4.0, 4.0)
    diag = jnp.exp(jax.random.uniform(key_diag, shape, jnp.float32, -0.69, 0.69))
    lower = jnp.where(row_index > col_index, off / jnp.sqrt(jnp.float32(NB)), 0.0)
    return (lower + jnp.where(row_index == col_index, diag, 0.0)).astype(jnp.float32)


def levels(key, extent, cuts, smallest, high):
    def one(position, blocks):
        draws = jax.random.uniform(jax.random.fold_in(jax.random.fold_in(key, 6), position), (blocks,), jnp.float32, smallest / len(cuts), high / len(cuts))
        return jnp.repeat(jnp.exp(draws), extent[position] // blocks).reshape((-1,) + (1,) * (len(extent) - position - 1))

    loudness = one(*cuts[0])
    for cut in cuts[1:]:
        loudness = loudness * one(*cut)
    return loudness


def normal_values(key, shape, deviation, most, pieces=(), kind=jnp.bfloat16):
    factor_of = levels(key, shape, pieces, -0.22, 0.18) if pieces else 1.0
    values = jax.random.normal(key, shape, jnp.float32) * deviation * factor_of
    return jnp.minimum(jnp.maximum(values, -most), most).astype(kind)


def setup_inputs(seed: int = 0) -> dict:
    splits = jax.random.split(jax.random.key(seed), 5)
    step = jax.random.randint(splits[0], (1,), 0, min(N_COL, BLK_DEV * N_ROW) - STEPS + 1).astype(jnp.int32)
    rhs = normal_values(splits[1], (ROWS, K), 1.0, 6.0, ((0, 8), (1, 32)), jnp.float32)
    panels = normal_values(splits[2], (ROWS, NB * N_COL), NB ** -0.5, 0.375, ((0, 8), (1, 32)), jnp.float32)
    diag_inverses = draw_diag_inverses(jax.random.fold_in(splits[4], 71), 0)
    return {"step": step, "rhs": rhs, "panels": panels, "diag_inverses": diag_inverses}


def reference(step, rhs, panels, diag_inverses):
    blocks = BLK_DEV * N_ROW
    y = rhs.reshape(N_ROW, BLK_DEV, NB, K).transpose(1, 0, 2, 3).reshape(blocks, NB, K)
    factor = panels.reshape(N_ROW, BLK_DEV, NB, N_COL, NB).transpose(1, 0, 2, 3, 4).reshape(blocks, NB, N_COL, NB)
    index = jnp.arange(blocks, dtype=jnp.int32)
    start = step[0].astype(jnp.int32)
    for turn in range(STEPS):
        k = start + turn
        inverse = lax.dynamic_slice_in_dim(diag_inverses, (k * NB).astype(jnp.int32), NB, 1)
        block_k = lax.dynamic_index_in_dim(y, k, 0, keepdims=False)
        solved = jnp.dot(inverse, block_k, precision=lax.Precision.HIGHEST, preferred_element_type=jnp.float32)
        column = lax.dynamic_index_in_dim(factor, k, 2, keepdims=False)
        change = jnp.einsum("bij,jk->bik", column, solved, precision=lax.Precision.HIGHEST)
        y = jnp.where((index > k)[:, None, None], y - change, y)
        y = jnp.where((index == k)[:, None, None], solved[None], y)
    return y.reshape(BLK_DEV, N_ROW, NB, K).transpose(1, 0, 2, 3).reshape(N_ROW * BLK_DEV * NB, K)
```

```python
import functools

import jax
import jax.numpy as jnp
from jax import lax
from jax.experimental import pallas as pl
from jax.experimental.pallas import tpu as pltpu
from jax.sharding import PartitionSpec as P

STEPS = 4
NB = 256
BLK = 6
N_START = 29
MESH = pl.DeviceIdType.MESH
SPLIT = 640
WIDE = 1024
REST = WIDE - SPLIT
SEGMENTS = [
    [(True, 0, 0, 256)],
    [(True, 256, 0, 256)],
    [(True, 512, 0, 128), (False, 0, 128, 128)],
    [(False, 128, 0, 256)],
]
WAYS = (-1, -1, 1, 1)


def device(x, core, y, z):
    return (lax.rem(x + 8, 4) * 2 + core, lax.rem(y + 8, 4) * 8 + lax.rem(z + 16, 8))


def halve(value):
    high = value.astype(jnp.bfloat16)
    return high, (value - high.astype(jnp.float32)).astype(jnp.bfloat16)


def product(a, b):
    dot = functools.partial(
        lax.dot_general, dimension_numbers=(((1,), (1,)), ((), ())), preferred_element_type=jnp.float32)
    return dot(a[0], b[0]) + (dot(a[0], b[1]) + dot(a[1], b[0]))


def step_kernel(start, panels, diag, rhs, out, a0, b0, a1, b1, stage0, stage1, ysel, tri_a, tri_b,
                solved, high, low, f_high, f_low, v_high, v_low, acc, send, recv, local):
    q, e = start // 8, start % 8
    owners = [((e + i) // 8 + q, (e + i) % 8) for i in range(STEPS)]
    row, col = lax.axis_index("row"), lax.axis_index("col")
    x, core = row // 2, lax.rem(row, 2)
    y, z = col // 8, lax.rem(col, 8)
    used = [0]

    def take(n=1):
        used[0] += n
        return used[0] - n

    def remote(src, dst, index, target):
        return pltpu.make_async_remote_copy(
            src_ref=src, dst_ref=dst, send_sem=send.at[index], recv_sem=recv.at[index],
            device_id=target, device_id_type=MESH)

    def at(dy=0, dz=0):
        return device(x, core, y + dy, z + dz)

    here = (row, col)

    barrier = pltpu.get_barrier_semaphore()
    friends = [at(dy=d) for d in (1, -1, 2)] + [at(dz=d) for d in range(1, 8)]
    friends += [device(x + d, c, y, z) for d in (1, -1) for c in (0, 1)] + [device(x, 1 - core, y, z)]
    for friend in friends:
        pl.semaphore_signal(barrier, inc=1, device_id=friend, device_id_type=MESH)

    loads = [pltpu.make_async_copy(rhs.at[:, pl.ds(NB * l, NB)], acc.at[:, pl.ds(NB * l, NB)], local.at[l])
             for l in range(BLK)]
    for load in loads:
        load.start()
    pl.semaphore_wait(barrier, len(friends))

    class Chunk:
        def __init__(self, a, b, stage, parts, number):
            self.a, self.b, self.stage, self.parts = a, b, stage, parts
            self.ysem = [[take() for _ in parts] for _ in range(3)]
            self.zsend = take(7 * 2)
            self.zrecv = [[take() for _ in SEGMENTS[i]] for i in range(STEPS)]
            self.sent = []
            self.a_z, self.a_y, self.a_far, self.b_y, self.b_z = {}, {}, [], [], {}
            self.local = number

        def spread_y(self):
            for i, (oy, oz) in enumerate(owners):
                @pl.when((y == oy) & (z == oz))
                def _(oy=oy):
                    for copy in self.outs(oy):
                        copy.start()
                    for copy in self.keeps(oy):
                        copy.start()

        def outs(self, oy):
            copies = []
            for k, d in enumerate((1, -1, 2)):
                ty = (oy + d) % 4
                for p, (ref, first, place, n) in enumerate(self.parts):
                    copies.append(remote(ref.at[pl.ds(first, n), ty], self.stage.at[pl.ds(place, n)],
                                         self.ysem[k][p], at(dy=d)))
            return copies

        def keeps(self, oy):
            return [pltpu.make_async_copy(ref.at[pl.ds(first, n), oy], self.stage.at[pl.ds(place, n)],
                                          local.at[6 + 2 * self.local + p])
                    for p, (ref, first, place, n) in enumerate(self.parts)]

        def target(self, i, seg, tz):
            in_a, lane, _, n = SEGMENTS[i][seg]
            if in_a:
                return self.a.at[y, tz, :, :, pl.ds(lane, n)]
            return self.b.at[tz, y, :, :, pl.ds(lane, n)]

        def pieces(self, i, tz, index):
            copies = []
            for seg, (_, _, lane, n) in enumerate(SEGMENTS[i]):
                copies.append(pltpu.make_async_remote_copy(
                    src_ref=self.stage.at[:, tz, :, pl.ds(lane, n)], dst_ref=self.target(i, seg, tz),
                    send_sem=send.at[self.zsend + 2 * index + seg], recv_sem=recv.at[self.zrecv[i][seg]],
                    device_id=(row, y * 8 + tz), device_id_type=MESH))
            return copies

        def own(self, i):
            return [pltpu.make_async_copy(self.stage.at[:, z, :, pl.ds(lane, n)], self.target(i, seg, z),
                                          local.at[10 + 2 * self.local + seg])
                    for seg, (_, _, lane, n) in enumerate(SEGMENTS[i])]

        def spread_z(self):
            for i, (oy, oz) in enumerate(owners):
                @pl.when(z == oz)
                def _(i=i, oy=oy):
                    @pl.when(y == oy)
                    def _():
                        for copy in self.keeps(oy):
                            copy.wait()
                    for k, d in enumerate((1, -1, 2)):
                        @pl.when(y == (oy + d) % 4)
                        def _(k=k):
                            for p, (ref, first, place, n) in enumerate(self.parts):
                                remote(ref.at[pl.ds(first, n), y], self.stage.at[pl.ds(place, n)],
                                       self.ysem[k][p], here).wait_recv()
                    for copy in self.own(i):
                        copy.start()

                    def one(k, carry):
                        for copy in self.pieces(i, lax.rem(z + k + 1, 8), k):
                            copy.start()
                        return carry
                    lax.fori_loop(0, 7, one, 0)

        def arrive(self):
            for i, (oy, oz) in enumerate(owners):
                @pl.when(z == oz)
                def _(i=i):
                    for copy in self.own(i):
                        copy.wait()

                @pl.when(z != oz)
                def _(i=i):
                    for copy in self.pieces(i, z, 0):
                        copy.wait_recv()

        def push(self, ref, dy, dz):
            copy = remote(ref, ref, take(), at(dy=dy, dz=dz))
            copy.start()
            self.sent.append(copy)
            return copy

        def send_a_z(self, t):
            right, left = lax.rem(z - (t - 1) + 8, 8), lax.rem(z + (t - 1), 8)
            if t < 4:
                lanes = (pl.ds(0, SPLIT), pl.ds(0, SPLIT))
            else:
                lanes = (pl.ds(0, 384), pl.ds(384, SPLIT - 384))
            self.a_z[t] = [self.push(self.a.at[y, right, :, :, lanes[0]], 0, 1),
                           self.push(self.a.at[y, left, :, :, lanes[1]], 0, -1)]

        def send_b_z(self, t):
            right, left = lax.rem(z - (t - 1) + 8, 8), lax.rem(z + (t - 1), 8)
            rows = (pl.ds(0, 4), pl.ds(0, 4)) if t < 4 else (pl.ds(0, 2), pl.ds(2, 2))
            self.b_z[t] = [self.push(self.b.at[right, rows[0]], 0, 1), self.push(self.b.at[left, rows[1]], 0, -1)]

        def send_a_y(self, t):
            origins = [lax.rem(z - t + 8, 8), lax.rem(z + t, 8)]
            if t in (0, 4):
                origins = origins[:1]
            self.a_y[t] = [self.push(self.a.at[y, o], d, 0) for o in origins for d in (1, -1)]

        def send_a_far(self, t):
            below, above = lax.rem(y + 3, 4), lax.rem(y + 1, 4)
            if t < 4:
                self.a_far.append(self.push(self.a.at[below, lax.rem(z - t + 8, 8)], 1, 0))
            if t > 0:
                self.a_far.append(self.push(self.a.at[above, lax.rem(z + t, 8)], -1, 0))

        def begin(self):
            self.send_a_z(1)
            self.b_y = [self.push(self.b.at[z, y], d, 0) for d in (1, -1, 2)]
            self.send_a_y(0)

        def arrived(self, copies):
            for copy in copies:
                copy.wait_recv()

        def step(self, t):
            if t <= 4:
                self.arrived(self.a_z[t])
                if t < 4:
                    self.send_a_z(t + 1)
                self.send_a_y(t)
            self.arrived(self.b_y if t == 1 else self.b_z[t - 1])
            if t <= 4:
                self.send_b_z(t)
            self.arrived(self.a_y[t - 1])
            self.send_a_far(t - 1)

        def end(self):
            self.arrived(self.a_far)

        def finish(self):
            for copy in self.sent:
                copy.wait_send()
            for i, (oy, oz) in enumerate(owners):
                @pl.when(z == oz)
                def _(i=i, oy=oy):
                    @pl.when(y == oy)
                    def _():
                        for copy in self.outs(oy):
                            copy.wait_send()

                    def one(k, carry):
                        for copy in self.pieces(i, lax.rem(z + k + 1, 8), k):
                            copy.wait_send()
                        return carry
                    lax.fori_loop(0, 7, one, 0)

    class Item:
        def __init__(self, i, parts, number):
            self.x, self.c = owners[i][1] // 2, owners[i][1] % 2
            self.parts = parts
            self.base = take(8 * len(parts))
            self.way = WAYS[i]
            self.side = lax.rem(x - self.x + 4, 4)
            self.owner = (x == self.x) & (core == self.c)
            self.local = number

        def each(self, h):
            for p, (src, dst) in enumerate(self.parts):
                yield self.base + 8 * p, src(h), dst(h)

        def outward(self):
            copies = []
            for h in (0, 1):
                for base, src, dst in self.each(h):
                    for k, d in enumerate((1, -1)):
                        copies.append(remote(src, dst, base + 2 * h + k, device((self.x + d) % 4, h, y, z)))
            for h in (0, 1):
                for base, src, dst in self.each(h):
                    copies.append(remote(src, dst, base + 4 + h, device(x, 1 - core, y, z)))
            return copies

        def kept(self):
            return [pltpu.make_async_copy(src, dst, local.at[self.local + 2 * p + h])
                    for h in (0, 1) for p, (_, src, dst) in enumerate(self.each(h))]

        def across(self, h):
            return [remote(dst, dst, base + 4 + h, device(x, 1 - core, y, z)) for base, _, dst in self.each(h)]

        def onward(self, h):
            return [remote(dst, dst, base + 6 + h, device((self.x + 2) % 4, h, y, z))
                    for base, _, dst in self.each(h)]

        def begin(self):
            @pl.when(self.owner)
            def _():
                for copy in self.outward() + self.kept():
                    copy.start()

        def relay(self):
            for h in (0, 1):
                for k, d in enumerate((1, -1)):
                    @pl.when((self.side == d % 4) & (core == h))
                    def _(h=h, k=k, d=d):
                        for base, src, dst in self.each(h):
                            remote(src, dst, base + 2 * h + k, here).wait_recv()
                        if d == self.way:
                            for copy in self.onward(h):
                                copy.start()
                        for copy in self.across(h):
                            copy.start()

        def far(self):
            for h in (0, 1):
                @pl.when((self.side == 2) & (core == h))
                def _(h=h):
                    for copy in self.onward(h):
                        copy.wait_recv()
                    for copy in self.across(h):
                        copy.start()

        def arrive(self):
            @pl.when(self.owner)
            def _():
                for copy in self.kept():
                    copy.wait()

            @pl.when((self.side == 0) & (core == 1 - self.c))
            def _():
                for h in (0, 1):
                    for copy in self.across(h):
                        copy.wait_recv()
            for h in (0, 1):
                @pl.when((self.side != 0) & (core == 1 - h))
                def _(h=h):
                    for copy in self.across(h):
                        copy.wait_recv()

        def finish(self):
            @pl.when(self.owner)
            def _():
                for copy in self.outward():
                    copy.wait_send()
            for h in (0, 1):
                @pl.when((self.side != 0) & (core == h))
                def _(h=h):
                    for copy in self.across(h):
                        copy.wait_send()

                @pl.when((self.side == self.way % 4) & (core == h))
                def _(h=h):
                    for copy in self.onward(h):
                        copy.wait_send()

    c0 = Chunk(a0, b0, stage0, [(diag, 0, 0, 1), (panels, q, 1, 2)], 0)
    c1 = Chunk(a1, b1, stage1, [(panels, q + 2, 0, 4 - q)], 1)
    half = rhs.shape[0] // 2
    yitems, titems = [], []
    for i, (l, _) in enumerate(owners):
        src = lambda h, l=l: rhs.at[pl.ds(half * h, half), pl.ds(NB * l, NB)]
        dst = lambda h, i=i: ysel.at[pl.ds(half * h, half), pl.ds(NB * i, NB)]
        yitems.append(Item(i, [(src, dst)], 14 + 2 * i))
    for i, (l, _) in enumerate(owners):
        if not i:
            continue
        p = l - q + 1
        n = min(NB * i, SPLIT)
        parts = [(lambda h, p=p, n=n: a0.at[pl.ds(2 * h, 2), :, p, :, pl.ds(0, n)],
                  lambda h, i=i, n=n: tri_a.at[i - 1, pl.ds(2 * h, 2), :, :, pl.ds(0, n)])]
        if NB * i > SPLIT:
            parts.append((lambda h, p=p: b0.at[pl.ds(4 * h, 4), :, p, :, pl.ds(0, 128)],
                          lambda h: tri_b.at[pl.ds(4 * h, 4)]))
        titems.append(Item(i, parts, 22 + 4 * (i - 1)))

    def assemble(part_a, part_b, keep, width=WIDE):
        for ty in range(4):
            rows = pl.ds(64 * ty, 64)
            n = min(width, SPLIT)
            value = part_a(ty, n).reshape(64, n)
            for lane in range(0, n, NB):
                m = min(NB, n - lane)
                f_high[rows, pl.ds(lane, m)], f_low[rows, pl.ds(lane, m)] = halve(
                    keep(lane, value[:, lane:lane + m]))
            if width > SPLIT:
                m = width - SPLIT
                value = part_b(ty, m).reshape(64, m)
                for lane in range(0, m, 128):
                    place = pl.ds(SPLIT + lane, 128)
                    f_high[rows, place], f_low[rows, place] = halve(keep(SPLIT + lane, value[:, lane:lane + 128]))

    everything = lambda lane, value: value

    def inverses():
        assemble(lambda ty, n: a0[ty, :, 0, :, :], lambda ty, m: b0[:, ty, 0, :, :], everything)
        v_high[...] = f_high[...]
        v_low[...] = f_low[...]

    def solve(i):
        lanes = pl.ds(NB * i, NB)
        right = ysel[:, lanes]
        if i:
            n = NB * i
            assemble(lambda ty, m: tri_a[i - 1, ty, :, :, pl.ds(0, m)], lambda ty, m: tri_b[:, ty], everything, n)
            right = right - product((high[:, pl.ds(0, n)], low[:, pl.ds(0, n)]),
                                    (f_high[:, pl.ds(0, n)], f_low[:, pl.ds(0, n)]))
        value = product(halve(right), (v_high[:, lanes], v_low[:, lanes]))
        solved[:, lanes] = value
        high[:, lanes], low[:, lanes] = halve(value)

    def store(l):
        return pltpu.make_async_copy(acc.at[:, pl.ds(NB * l, NB)], out.at[:, pl.ds(NB * l, NB)], local.at[40 + l])

    def update(chunk, p, l):
        block = l * 8 + row
        lanes = pl.ds(NB * l, NB)

        def keep(lane, value):
            if l >= q + 2:
                return value
            return jnp.where(start + lane // NB < block, value, 0.0)
        assemble(lambda ty, n: chunk.a[ty, :, p, :, :], lambda ty, m: chunk.b[:, ty, p, :, :], keep)
        acc[:, lanes] = acc[:, lanes] - product((high[...], low[...]), (f_high[...], f_low[...]))
        for i in range(STEPS):
            if owners[i][0] == l:
                @pl.when(block == start + i)
                def _(i=i):
                    acc[:, lanes] = solved[:, pl.ds(NB * i, NB)]
        store(l).start()

    c0.spread_y()
    for item in yitems:
        item.begin()
    c1.spread_y()
    c0.spread_z()
    for load in loads:
        load.wait()
    for l in range(q):
        store(l).start()
    c0.arrive()
    c0.begin()
    c1.spread_z()
    for t in (1, 2, 3):
        c0.step(t)
    for item in yitems:
        item.relay()
    c0.step(4)
    c1.arrive()
    c1.begin()
    c0.step(5)
    for item in yitems:
        item.far()
    c0.end()
    for item in titems:
        item.begin()
    c1.step(1)
    c1.step(2)
    for item in titems:
        item.relay()
    inverses()
    for item in yitems:
        item.arrive()
    solve(0)
    c1.step(3)
    for item in titems:
        item.far()
    c1.step(4)
    for i in range(1, STEPS):
        titems[i - 1].arrive()
        solve(i)
    c1.step(5)
    update(c0, 1, q)
    update(c0, 2, q + 1)
    c1.end()
    for l in range(q + 2, BLK):
        update(c1, l - q - 2, l)
    for item in yitems + titems:
        item.finish()
    c0.finish()
    c1.finish()
    for l in range(BLK):
        store(l).wait()
    assert used[0] <= send.shape[0], used[0]


def run(start, panels, diag, rhs):
    cols = rhs.shape[0]
    n = BLK - 2 - start // 8
    anywhere = pl.BlockSpec(memory_space=pl.ANY)
    f32, bf16 = jnp.float32, jnp.bfloat16
    return pl.pallas_call(
        functools.partial(step_kernel, start),
        out_shape=jax.ShapeDtypeStruct(rhs.shape, f32),
        in_specs=[anywhere] * 3,
        out_specs=anywhere,
        scratch_shapes=[
            pltpu.VMEM((4, 8, 3, 8, SPLIT), f32),
            pltpu.VMEM((8, 4, 3, 8, REST), f32),
            pltpu.VMEM((4, 8, n, 8, SPLIT), f32),
            pltpu.VMEM((8, 4, n, 8, REST), f32),
            pltpu.VMEM((3, 8, 8, NB), f32),
            pltpu.VMEM((n, 8, 8, NB), f32),
            pltpu.VMEM((cols, WIDE), f32),
            pltpu.VMEM((STEPS - 1, 4, 8, 8, SPLIT), f32),
            pltpu.VMEM((8, 4, 8, 128), f32),
            pltpu.VMEM((cols, WIDE), f32),
            pltpu.VMEM((cols, WIDE), bf16),
            pltpu.VMEM((cols, WIDE), bf16),
            pltpu.VMEM((NB, WIDE), bf16),
            pltpu.VMEM((NB, WIDE), bf16),
            pltpu.VMEM((NB, WIDE), bf16),
            pltpu.VMEM((NB, WIDE), bf16),
            pltpu.VMEM((cols, BLK * NB), f32),
            pltpu.SemaphoreType.DMA((256,)),
            pltpu.SemaphoreType.DMA((256,)),
            pltpu.SemaphoreType.DMA((48,)),
        ],
        compiler_params=pltpu.CompilerParams(
            collective_id=start, has_side_effects=True, vmem_limit_bytes=48 * 2**20),
        name=f"steps_{start}",
    )(panels, diag, rhs)


def body(step, rhs, panels, diag_inverses):
    parts = panels.reshape(BLK, 4, 8, 8, NB)
    inverse = diag_inverses.reshape(1, 4, 8, 8, NB)
    branches = [functools.partial(run, s) for s in range(N_START)]
    return lax.switch(step[0], branches, parts, inverse, rhs.T).T


def solution(mesh):
    in_specs = (P(), P("row", "col"), P("row", "col"), P(None, "col"))
    out_specs = P("row", "col")
    return jax.shard_map(body, mesh=mesh, in_specs=in_specs, out_specs=out_specs, check_vma=False)
```

```python
import functools

import jax
import jax.numpy as jnp
from jax import lax
from jax.experimental import pallas as pl
from jax.experimental.pallas import tpu as pltpu
from jax.sharding import PartitionSpec as P

STEPS = 4
NB = 256
BLK = 6
MESH = pl.DeviceIdType.MESH
SPLIT = 640
WIDE = 1024
REST = WIDE - SPLIT
SEGMENTS = [
    [(True, 0, 0, 256)],
    [(True, 256, 0, 256)],
    [(True, 512, 0, 128), (False, 0, 128, 128)],
    [(False, 128, 0, 256)],
]
PAIRS = [(1, 0), (2, 0), (2, 1), (3, 0), (3, 1), (3, 2)]


def device(x, core, y, z):
    return (lax.rem(x + 8, 4) * 2 + core, lax.rem(y + 8, 4) * 8 + lax.rem(z + 16, 8))


def halve(value):
    high = value.astype(jnp.bfloat16)
    return high, (value - high.astype(jnp.float32)).astype(jnp.bfloat16)


def product(a, b):
    dot = functools.partial(
        lax.dot_general, dimension_numbers=(((1,), (1,)), ((), ())), preferred_element_type=jnp.float32)
    return dot(a[0], b[0]) + (dot(a[0], b[1]) + dot(a[1], b[0]))


def choose(index, values):
    result = values[0]
    for n, value in enumerate(values[1:], 1):
        result = jnp.where(index == n, value, result)
    return result


def step_kernel(step, panels, diag, rhs, out, r0, r1, r2, s0, s1, s2, p0, p1, p2, a1, b1, a2, b2, gathered,
                tc, tall, ycand, ypart, yhalf, ysel, solved, high, low, f_high, f_low, acc, send, recv,
                local):
    start = step[0]
    row, col = lax.axis_index("row"), lax.axis_index("col")
    x, core = row // 2, lax.rem(row, 2)
    y, z = col // 8, lax.rem(col, 8)
    row_step = lax.rem(row - start + 32, 4)
    row_block = start + row_step
    row_local = row_block // 8
    row_real = lax.rem(row_block, 8) == row
    col_block = start + lax.rem(z - start + 32, 4)
    col_y = col_block // 8
    used = [0]
    sent = []

    def take(n=1):
        used[0] += n
        return used[0] - n

    def remote(src, dst, index, target):
        return pltpu.make_async_remote_copy(
            src_ref=src, dst_ref=dst, send_sem=send.at[index], recv_sem=recv.at[index],
            device_id=target, device_id_type=MESH)

    def push(src, dst, target):
        copy = remote(src, dst, take(), target)
        copy.start()
        sent.append(copy)
        return copy

    def arrived(copies):
        for copy in copies:
            copy.wait_recv()

    def at(dy=0, dz=0):
        return device(x, core, y + dy, z + dz)

    def across(dx=0, dc=0):
        return device(x + dx, lax.rem(core + dc, 2), y, z)

    barrier = pltpu.get_barrier_semaphore()
    others = [(dx, dc) for dx in range(4) for dc in (0, 1) if dx or dc]
    friends = [at(dy=d) for d in (1, -1, 2)] + [at(dz=d) for d in range(1, 8)] + [across(*o) for o in others]
    for friend in friends:
        pl.semaphore_signal(barrier, inc=1, device_id=friend, device_id_type=MESH)
    loads = [pltpu.make_async_copy(rhs.at[:, pl.ds(NB * l, NB)], acc.at[:, pl.ds(NB * l, NB)], local.at[l])
             for l in range(BLK)]
    for load in loads:
        load.start()
    tc[0] = diag[0]
    for ty in range(4):
        tc[1, ty] = choose(row_local, [panels[l, ty] for l in range(4)])
    pl.semaphore_wait(barrier, len(friends))

    class Scatter:
        def __init__(self, src, first, n, landing, stage, landed):
            self.src, self.first, self.n = src, first, n
            self.landing, self.stage, self.landed = landing, stage, landed

        def along_y(self):
            blocks = pl.ds(self.first, self.n)
            self.copies = [push(self.src.at[blocks, lax.rem(y + d + 4, 4)], self.landing.at[k], at(dy=d))
                           for k, d in enumerate((1, -1, 2))]

        def along_z(self):
            arrived(self.copies)
            back = lax.rem(y - col_y + 4, 4)
            for p in range(self.n):
                for tz in range(8):
                    self.stage[tz, p] = choose(back, [self.src[self.first + p, y, tz]] + [
                        self.landing[k, p, tz] for k in (0, 2, 1)])
            self.copies = [push(self.stage.at[lax.rem(z + d, 8)], self.landed.at[z], at(dz=d)) for d in range(1, 8)]
            self.landed[z] = self.stage[z]

        def arrive(self):
            arrived(self.copies)

        def pick(self, i, p):
            return choose(lax.rem(start + i, 8), [self.landed[n, p] for n in range(8)])

    class Chunk:
        def __init__(self, a, b, width, cut):
            self.a, self.b, self.width, self.cut = a, b, width, cut
            self.a_z, self.a_y, self.a_far, self.b_y, self.b_z = {}, {}, [], [], {}

        def move(self, ref, dy, dz):
            return push(ref, ref, at(dy=dy, dz=dz))

        def send_a_z(self, t):
            right, left = lax.rem(z - (t - 1) + 8, 8), lax.rem(z + (t - 1), 8)
            if t < 4:
                lanes = (pl.ds(0, self.width), pl.ds(0, self.width))
            else:
                lanes = (pl.ds(0, self.cut), pl.ds(self.cut, self.width - self.cut))
            self.a_z[t] = [self.move(self.a.at[y, right, :, :, lanes[0]], 0, 1),
                           self.move(self.a.at[y, left, :, :, lanes[1]], 0, -1)]

        def send_b_z(self, t):
            right, left = lax.rem(z - (t - 1) + 8, 8), lax.rem(z + (t - 1), 8)
            rows = (pl.ds(0, 4), pl.ds(0, 4)) if t < 4 else (pl.ds(0, 2), pl.ds(2, 2))
            self.b_z[t] = [self.move(self.b.at[right, rows[0]], 0, 1), self.move(self.b.at[left, rows[1]], 0, -1)]

        def send_a_y(self, t):
            origins = [lax.rem(z - t + 8, 8), lax.rem(z + t, 8)]
            if t in (0, 4):
                origins = origins[:1]
            self.a_y[t] = [self.move(self.a.at[y, o], d, 0) for o in origins for d in (1, -1)]

        def send_a_far(self, t):
            below, above = lax.rem(y + 3, 4), lax.rem(y + 1, 4)
            if t < 4:
                self.a_far.append(self.move(self.a.at[below, lax.rem(z - t + 8, 8)], 1, 0))
            if t > 0:
                self.a_far.append(self.move(self.a.at[above, lax.rem(z + t, 8)], -1, 0))

        def begin(self):
            self.send_a_z(1)
            if self.b is not None:
                self.b_y = [self.move(self.b.at[z, y], d, 0) for d in (1, -1, 2)]
            self.send_a_y(0)

        def step(self, t):
            if t <= 4:
                arrived(self.a_z[t])
                if t < 4:
                    self.send_a_z(t + 1)
                self.send_a_y(t)
            if self.b is not None:
                arrived(self.b_y if t == 1 else self.b_z[t - 1])
                if t <= 4:
                    self.send_b_z(t)
            arrived(self.a_y[t - 1])
            self.send_a_far(t - 1)

        def end(self):
            arrived(self.a_far)

    small = Scatter(tc, 0, 2, r0, s0, p0)
    first = Scatter(panels, 0, 3, r1, s1, p1)
    second = Scatter(panels, 3, 3, r2, s2, p2)
    g = Chunk(gathered.at[core], None, NB, 128)
    c1 = Chunk(a1, b1, SPLIT, 384)
    c2 = Chunk(a2, b2, SPLIT, 384)

    def place(scatter, a, b):
        for i in range(STEPS):
            for p in range(3):
                value = scatter.pick(i, p)
                for in_a, lane, source, n in SEGMENTS[i]:
                    part = value[:, source:source + n]
                    if in_a:
                        a[y, z, p, :, lane:lane + n] = part
                    else:
                        b[z, y, p, :, lane:lane + n] = part

    half = rhs.shape[0] // 2
    side = x // 2

    def candidates():
        for load in loads:
            load.wait()
        for h in (0, 1):
            ycand[h] = choose(row_local, [acc[pl.ds(half * h, half), pl.ds(NB * l, NB)] for l in range(4)])
        return push(ycand.at[1 - side], ypart, across(dx=2))

    def share(copy):
        arrived([copy])
        yhalf[...] = jnp.where(row_real, ycand[side], ypart[...])
        slot = lax.rem(row, 4)
        copies = [push(yhalf, ysel.at[slot, side], across(dx=d)) for d in (1, 3, 2)]
        copies.append(push(yhalf, ysel.at[slot, side], across(dc=1)))
        ysel[slot, side] = yhalf[...]
        return copies

    def relay(copies):
        arrived(copies[:3])
        passed = []
        for d in (1, 3, 2):
            sx = lax.rem(x - d + 4, 4)
            ref = ysel.at[lax.rem(2 * sx + core, 4), sx // 2]
            passed.append(push(ref, ref, across(dc=1)))
        return [copies[3]] + passed

    def triangle():
        for i in range(STEPS):
            tall[row, i] = small.pick(i, 1)
        return [push(tall.at[row], tall.at[row], across(*o)) for o in others]

    def payload():
        for m in range(2):
            gathered[core, y, z, m] = small.pick(2 * core + m, 0)
        for m in range(3):
            i = jnp.where(core == 0, PAIRS[m][0], PAIRS[3 + m][0])
            j = jnp.where(core == 0, PAIRS[m][1], PAIRS[3 + m][1])
            gathered[core, y, z, 2 + m] = choose(lax.rem(start + i, 8), [tall[n, j] for n in range(8)])

    def square(c, m):
        return halve(gathered[c, :, :, m].reshape(NB, NB))

    def solve(i):
        lanes = pl.ds(NB * i, NB)
        right = choose(lax.rem(start + i, 4), [ysel[n].reshape(2 * half, NB) for n in range(4)])
        for index, (k, j) in enumerate(PAIRS):
            if k == i:
                before = pl.ds(NB * j, NB)
                right = right - product((high[:, before], low[:, before]), square(index // 3, 2 + index % 3))
        value = product(halve(right), square(i // 2, i % 2))
        solved[...] = value if i == 0 else jnp.where(row_step == i, value, solved[...])
        high[:, lanes], low[:, lanes] = halve(value)

    def assemble(chunk, p, block):
        for ty in range(4):
            rows = pl.ds(64 * ty, 64)
            for i in range(STEPS):
                keep = start + i < block
                for in_a, lane, source, n in SEGMENTS[i]:
                    if in_a:
                        value = chunk.a[ty, :, p, :, lane:lane + n]
                    else:
                        value = chunk.b[:, ty, p, :, lane:lane + n]
                    value = jnp.where(keep, value.reshape(64, n), 0.0)
                    to = pl.ds(NB * i + source, n)
                    f_high[rows, to], f_low[rows, to] = halve(value)

    def store(l):
        return pltpu.make_async_copy(acc.at[:, pl.ds(NB * l, NB)], out.at[:, pl.ds(NB * l, NB)], local.at[8 + l])

    def update(chunk, p, l):
        assemble(chunk, p, l * 8 + row)
        lanes = pl.ds(NB * l, NB)
        value = acc[:, lanes] - product((high[...], low[...]), (f_high[...], f_low[...]))
        if l < 4:
            value = jnp.where(row_real & (row_local == l), solved[...], value)
        acc[:, lanes] = value
        store(l).start()

    small.along_y()
    first.along_y()
    second.along_y()
    ycopy = candidates()
    small.along_z()
    first.along_z()
    small.arrive()
    tcopies = triangle()
    ycopies = share(ycopy)
    first.arrive()
    place(first, a1, b1)
    arrived(tcopies)
    payload()
    g.begin()
    c1.begin()
    second.along_z()
    g.step(1)
    c1.step(1)
    g.step(2)
    g.step(3)
    c1.step(2)
    g.step(4)
    second.arrive()
    place(second, a2, b2)
    g.step(5)
    c1.step(3)
    g.end()
    gcopy = push(gathered.at[core], gathered.at[core], across(dc=1))
    yrelays = relay(ycopies)
    c1.step(4)
    c2.begin()
    c1.step(5)
    arrived([gcopy] + yrelays)
    solve(0)
    c2.step(1)
    solve(1)
    solve(2)
    c2.step(2)
    solve(3)
    c1.end()
    c2.step(3)
    update(c1, 0, 0)
    c2.step(4)
    update(c1, 1, 1)
    c2.step(5)
    update(c1, 2, 2)
    c2.end()
    for l in range(3, BLK):
        update(c2, l - 3, l)
    for copy in sent:
        copy.wait_send()
    for l in range(BLK):
        store(l).wait()
    assert used[0] <= send.shape[0], used[0]


def run(step, panels, diag, rhs):
    cols = rhs.shape[0]
    anywhere = pl.BlockSpec(memory_space=pl.ANY)
    inside = pl.BlockSpec(memory_space=pltpu.VMEM)
    f32, bf16 = jnp.float32, jnp.bfloat16
    shapes = [
        (4, 2, 8, 8, NB), (4, 3, 8, 8, NB), (4, 3, 8, 8, NB),
        (8, 2, 8, NB), (8, 3, 8, NB), (8, 3, 8, NB),
        (8, 2, 8, NB), (8, 3, 8, NB), (8, 3, 8, NB),
        (4, 8, 3, 8, SPLIT), (8, 4, 3, 8, REST), (4, 8, 3, 8, SPLIT), (8, 4, 3, 8, REST),
        (2, 4, 8, 5, 8, NB),
        (2, 4, 8, 8, NB), (8, 4, 8, NB),
        (2, cols // 2, NB), (cols // 2, NB), (cols // 2, NB), (STEPS, 2, cols // 2, NB),
        (cols, NB),
    ]
    return pl.pallas_call(
        step_kernel,
        out_shape=jax.ShapeDtypeStruct(rhs.shape, f32),
        in_specs=[pl.BlockSpec(memory_space=pltpu.SMEM), inside, inside, anywhere],
        out_specs=anywhere,
        scratch_shapes=[pltpu.VMEM(shape, f32) for shape in shapes] + [
            pltpu.VMEM((cols, WIDE), bf16),
            pltpu.VMEM((cols, WIDE), bf16),
            pltpu.VMEM((NB, WIDE), bf16),
            pltpu.VMEM((NB, WIDE), bf16),
            pltpu.VMEM((cols, BLK * NB), f32),
            pltpu.SemaphoreType.DMA((224,)),
            pltpu.SemaphoreType.DMA((224,)),
            pltpu.SemaphoreType.DMA((16,)),
        ],
        compiler_params=pltpu.CompilerParams(
            collective_id=0, has_side_effects=True, vmem_limit_bytes=48 * 2**20),
        name="steps",
    )(step, panels, diag, rhs)


def body(step, rhs, panels, diag_inverses):
    parts = panels.reshape(BLK, 4, 8, 8, NB)
    inverse = diag_inverses.reshape(1, 4, 8, 8, NB)
    return run(step, parts, inverse, rhs.T).T


def solution(mesh):
    in_specs = (P(), P("row", "col"), P("row", "col"), P(None, "col"))
    out_specs = P("row", "col")
    return jax.shard_map(body, mesh=mesh, in_specs=in_specs, out_specs=out_specs, check_vma=False)
```

```python
import functools

import jax
import jax.numpy as jnp
from jax import lax
from jax.experimental import pallas as pl
from jax.experimental.pallas import tpu as pltpu
from jax.sharding import PartitionSpec as P

STEPS = 4
NB = 256
BLK = 6
MESH = pl.DeviceIdType.MESH
SPLIT = 640
WIDE = 1024
REST = WIDE - SPLIT
SEGMENTS = [
    [(True, 0, 0, 256)],
    [(True, 256, 0, 256)],
    [(True, 512, 0, 128), (False, 0, 128, 128)],
    [(False, 128, 0, 256)],
]
PAIRS = [(1, 0), (2, 0), (2, 1), (3, 0), (3, 1), (3, 2)]


def device(x, core, y, z):
    return (lax.rem(x + 8, 4) * 2 + core, lax.rem(y + 8, 4) * 8 + lax.rem(z + 16, 8))


def halve(value):
    high = value.astype(jnp.bfloat16)
    return high, (value - high.astype(jnp.float32)).astype(jnp.bfloat16)


def product(a, b):
    dot = functools.partial(
        lax.dot_general, dimension_numbers=(((1,), (1,)), ((), ())), preferred_element_type=jnp.float32)
    return dot(a[0], b[0]) + (dot(a[0], b[1]) + dot(a[1], b[0]))


def choose(index, values):
    result = values[0]
    for n, value in enumerate(values[1:], 1):
        result = jnp.where(index == n, value, result)
    return result


def step_kernel(step, factor, diag, rhs, acc, panels, r0, r1, r2, s0, s1, s2, p0, p1, p2, a1, b1, a2, b2, gathered,
                tc, tall, ycand, ypart, yhalf, ysel, solved, high, low, f_high, f_low, send, recv,
                local):
    start = step[0]
    row, col = lax.axis_index("row"), lax.axis_index("col")
    x, core = row // 2, lax.rem(row, 2)
    y, z = col // 8, lax.rem(col, 8)
    row_step = lax.rem(row - start + 32, 4)
    row_block = start + row_step
    row_local = row_block // 8
    row_real = lax.rem(row_block, 8) == row
    col_block = start + lax.rem(z - start + 32, 4)
    col_y = col_block // 8
    used = [0]
    sent = []

    def take(n=1):
        used[0] += n
        return used[0] - n

    def remote(src, dst, index, target):
        return pltpu.make_async_remote_copy(
            src_ref=src, dst_ref=dst, send_sem=send.at[index], recv_sem=recv.at[index],
            device_id=target, device_id_type=MESH)

    def push(src, dst, target):
        copy = remote(src, dst, take(), target)
        copy.start()
        sent.append(copy)
        return copy

    def arrived(copies):
        for copy in copies:
            copy.wait_recv()

    def at(dy=0, dz=0):
        return device(x, core, y + dy, z + dz)

    def across(dx=0, dc=0):
        return device(x + dx, lax.rem(core + dc, 2), y, z)

    barrier = pltpu.get_barrier_semaphore()
    others = [(dx, dc) for dx in range(4) for dc in (0, 1) if dx or dc]
    friends = [at(dy=d) for d in (1, -1, 2)] + [at(dz=d) for d in range(1, 8)] + [across(*o) for o in others]
    for friend in friends:
        pl.semaphore_signal(barrier, inc=1, device_id=friend, device_id_type=MESH)
    loads = [pltpu.make_async_copy(rhs.at[:, pl.ds(NB * l, NB)], acc.at[:, pl.ds(NB * l, NB)], local.at[l])
             for l in range(BLK)]
    fetches = [pltpu.make_async_copy(factor, panels, local.at[6]),
               pltpu.make_async_copy(diag, tc.at[pl.ds(0, 1)], local.at[7])]
    for load in fetches + loads:
        load.start()
    for fetch in fetches:
        fetch.wait()
    for ty in range(4):
        tc[1, ty] = choose(row_local, [panels[l, ty] for l in range(4)])
    pl.semaphore_wait(barrier, len(friends))

    class Scatter:
        def __init__(self, src, first, n, landing, stage, landed):
            self.src, self.first, self.n = src, first, n
            self.landing, self.stage, self.landed = landing, stage, landed

        def along_y(self):
            blocks = pl.ds(self.first, self.n)
            self.copies = [push(self.src.at[blocks, lax.rem(y + d + 4, 4)], self.landing.at[k], at(dy=d))
                           for k, d in enumerate((1, -1, 2))]

        def along_z(self):
            arrived(self.copies)
            back = lax.rem(y - col_y + 4, 4)
            for p in range(self.n):
                for tz in range(8):
                    self.stage[tz, p] = choose(back, [self.src[self.first + p, y, tz]] + [
                        self.landing[k, p, tz] for k in (0, 2, 1)])
            self.copies = [push(self.stage.at[lax.rem(z + d, 8)], self.landed.at[z], at(dz=d)) for d in range(1, 8)]
            self.landed[z] = self.stage[z]

        def arrive(self):
            arrived(self.copies)

        def pick(self, i, p):
            return choose(lax.rem(start + i, 8), [self.landed[n, p] for n in range(8)])

    class Chunk:
        def __init__(self, a, b, width, cut):
            self.a, self.b, self.width, self.cut = a, b, width, cut
            self.a_z, self.a_y, self.a_far, self.b_y, self.b_z = {}, {}, [], [], {}

        def move(self, ref, dy, dz):
            return push(ref, ref, at(dy=dy, dz=dz))

        def send_a_z(self, t):
            right, left = lax.rem(z - (t - 1) + 8, 8), lax.rem(z + (t - 1), 8)
            if t < 4:
                lanes = (pl.ds(0, self.width), pl.ds(0, self.width))
            else:
                lanes = (pl.ds(0, self.cut), pl.ds(self.cut, self.width - self.cut))
            self.a_z[t] = [self.move(self.a.at[y, right, :, :, lanes[0]], 0, 1),
                           self.move(self.a.at[y, left, :, :, lanes[1]], 0, -1)]

        def send_b_z(self, t):
            right, left = lax.rem(z - (t - 1) + 8, 8), lax.rem(z + (t - 1), 8)
            rows = (pl.ds(0, 4), pl.ds(0, 4)) if t < 4 else (pl.ds(0, 2), pl.ds(2, 2))
            self.b_z[t] = [self.move(self.b.at[right, rows[0]], 0, 1), self.move(self.b.at[left, rows[1]], 0, -1)]

        def send_a_y(self, t):
            origins = [lax.rem(z - t + 8, 8), lax.rem(z + t, 8)]
            if t in (0, 4):
                origins = origins[:1]
            self.a_y[t] = [self.move(self.a.at[y, o], d, 0) for o in origins for d in (1, -1)]

        def send_a_far(self, t):
            below, above = lax.rem(y + 3, 4), lax.rem(y + 1, 4)
            if t < 4:
                self.a_far.append(self.move(self.a.at[below, lax.rem(z - t + 8, 8)], 1, 0))
            if t > 0:
                self.a_far.append(self.move(self.a.at[above, lax.rem(z + t, 8)], -1, 0))

        def begin(self):
            self.send_a_z(1)
            if self.b is not None:
                self.b_y = [self.move(self.b.at[z, y], d, 0) for d in (1, -1, 2)]
            self.send_a_y(0)

        def step(self, t):
            if t <= 4:
                arrived(self.a_z[t])
                if t < 4:
                    self.send_a_z(t + 1)
                self.send_a_y(t)
            if self.b is not None:
                arrived(self.b_y if t == 1 else self.b_z[t - 1])
                if t <= 4:
                    self.send_b_z(t)
            arrived(self.a_y[t - 1])
            self.send_a_far(t - 1)

        def end(self):
            arrived(self.a_far)

    small = Scatter(tc, 0, 2, r0, s0, p0)
    first = Scatter(panels, 0, 3, r1, s1, p1)
    second = Scatter(panels, 3, 3, r2, s2, p2)
    g = Chunk(gathered.at[core], None, NB, 128)
    c1 = Chunk(a1, b1, SPLIT, 384)
    c2 = Chunk(a2, b2, SPLIT, 384)

    def place(scatter, a, b):
        for i in range(STEPS):
            for p in range(3):
                value = scatter.pick(i, p)
                for in_a, lane, source, n in SEGMENTS[i]:
                    part = value[:, source:source + n]
                    if in_a:
                        a[y, z, p, :, lane:lane + n] = part
                    else:
                        b[z, y, p, :, lane:lane + n] = part

    half = rhs.shape[0] // 2
    side = x // 2

    def candidates():
        for load in loads:
            load.wait()
        for h in (0, 1):
            ycand[h] = choose(row_local, [acc[pl.ds(half * h, half), pl.ds(NB * l, NB)] for l in range(4)])
        return push(ycand.at[1 - side], ypart, across(dx=2))

    def share(copy):
        arrived([copy])
        yhalf[...] = jnp.where(row_real, ycand[side], ypart[...])
        slot = lax.rem(row, 4)
        copies = [push(yhalf, ysel.at[slot, side], across(dx=d)) for d in (1, 3, 2)]
        copies.append(push(yhalf, ysel.at[slot, side], across(dc=1)))
        ysel[slot, side] = yhalf[...]
        return copies

    def relay(copies):
        arrived(copies[:3])
        passed = []
        for d in (1, 3, 2):
            sx = lax.rem(x - d + 4, 4)
            ref = ysel.at[lax.rem(2 * sx + core, 4), sx // 2]
            passed.append(push(ref, ref, across(dc=1)))
        return [copies[3]] + passed

    def triangle():
        for i in range(STEPS):
            tall[row, i] = small.pick(i, 1)
        return [push(tall.at[row], tall.at[row], across(*o)) for o in others]

    def payload():
        for m in range(2):
            gathered[core, y, z, m] = small.pick(2 * core + m, 0)
        for m in range(3):
            i = jnp.where(core == 0, PAIRS[m][0], PAIRS[3 + m][0])
            j = jnp.where(core == 0, PAIRS[m][1], PAIRS[3 + m][1])
            gathered[core, y, z, 2 + m] = choose(lax.rem(start + i, 8), [tall[n, j] for n in range(8)])

    def square(c, m):
        return halve(gathered[c, :, :, m].reshape(NB, NB))

    def solve(i):
        lanes = pl.ds(NB * i, NB)
        right = choose(lax.rem(start + i, 4), [ysel[n].reshape(2 * half, NB) for n in range(4)])
        for index, (k, j) in enumerate(PAIRS):
            if k == i:
                before = pl.ds(NB * j, NB)
                right = right - product((high[:, before], low[:, before]), square(index // 3, 2 + index % 3))
        value = product(halve(right), square(i // 2, i % 2))
        solved[...] = value if i == 0 else jnp.where(row_step == i, value, solved[...])
        high[:, lanes], low[:, lanes] = halve(value)

    def assemble(chunk, p, block):
        for ty in range(4):
            rows = pl.ds(64 * ty, 64)
            for i in range(STEPS):
                keep = start + i < block
                for in_a, lane, source, n in SEGMENTS[i]:
                    if in_a:
                        value = chunk.a[ty, :, p, :, lane:lane + n]
                    else:
                        value = chunk.b[:, ty, p, :, lane:lane + n]
                    value = jnp.where(keep, value.reshape(64, n), 0.0)
                    to = pl.ds(NB * i + source, n)
                    f_high[rows, to], f_low[rows, to] = halve(value)

    def update(chunk, p, l):
        assemble(chunk, p, l * 8 + row)
        lanes = pl.ds(NB * l, NB)
        value = acc[:, lanes] - product((high[...], low[...]), (f_high[...], f_low[...]))
        if l < 4:
            value = jnp.where(row_real & (row_local == l), solved[...], value)
        acc[:, lanes] = value

    small.along_y()
    first.along_y()
    second.along_y()
    small.along_z()
    ycopy = candidates()
    small.arrive()
    tcopies = triangle()
    first.along_z()
    arrived(tcopies)
    payload()
    g.begin()
    ycopies = share(ycopy)
    first.arrive()
    place(first, a1, b1)
    c1.begin()
    g.step(1)
    second.along_z()
    c1.step(1)
    g.step(2)
    second.arrive()
    place(second, a2, b2)
    c2.begin()
    g.step(3)
    c1.step(2)
    c2.step(1)
    g.step(4)
    c1.step(3)
    g.step(5)
    c2.step(2)
    g.end()
    gcopy = push(gathered.at[core], gathered.at[core], across(dc=1))
    c1.step(4)
    yrelays = relay(ycopies)
    c2.step(3)
    c1.step(5)
    arrived([gcopy] + yrelays)
    solve(0)
    solve(1)
    c2.step(4)
    solve(2)
    solve(3)
    c2.step(5)
    c1.end()
    update(c1, 0, 0)
    update(c1, 1, 1)
    update(c1, 2, 2)
    c2.end()
    update(c2,0,3)
    update(c2,1,4)
    update(c2,2,5)
    for copy in sent:
        copy.wait_send()
    assert used[0] <= send.shape[0], used[0]


def run(step, panels, diag, rhs):
    cols = rhs.shape[0]
    anywhere = pl.BlockSpec(memory_space=pl.ANY)
    inside = pl.BlockSpec(memory_space=pltpu.VMEM)
    f32, bf16 = jnp.float32, jnp.bfloat16
    shapes = [
        (BLK, 4, 8, 8, NB),
        (4, 2, 8, 8, NB), (4, 3, 8, 8, NB), (4, 3, 8, 8, NB),
        (8, 2, 8, NB), (8, 3, 8, NB), (8, 3, 8, NB),
        (8, 2, 8, NB), (8, 3, 8, NB), (8, 3, 8, NB),
        (4, 8, 3, 8, SPLIT), (8, 4, 3, 8, REST), (4, 8, 3, 8, SPLIT), (8, 4, 3, 8, REST),
        (2, 4, 8, 5, 8, NB),
        (2, 4, 8, 8, NB), (8, 4, 8, NB),
        (2, cols // 2, NB), (cols // 2, NB), (cols // 2, NB), (STEPS, 2, cols // 2, NB),
        (cols, NB),
    ]
    return pl.pallas_call(
        step_kernel,
        out_shape=pltpu.VMEM(rhs.shape, f32),
        in_specs=[pl.BlockSpec(memory_space=pltpu.SMEM), anywhere, anywhere, anywhere],
        out_specs=inside,
        scratch_shapes=[pltpu.VMEM(shape, f32) for shape in shapes] + [
            pltpu.VMEM((cols, WIDE), bf16),
            pltpu.VMEM((cols, WIDE), bf16),
            pltpu.VMEM((NB, WIDE), bf16),
            pltpu.VMEM((NB, WIDE), bf16),
            pltpu.SemaphoreType.DMA((224,)),
            pltpu.SemaphoreType.DMA((224,)),
            pltpu.SemaphoreType.DMA((16,)),
        ],
        compiler_params=pltpu.CompilerParams(
            collective_id=0, has_side_effects=True, vmem_limit_bytes=48 * 2**20),
        name="steps",
    )(step, panels, diag, rhs)


def body(step, rhs, panels, diag_inverses):
    parts = panels.reshape(BLK, 4, 8, 8, NB)
    inverse = diag_inverses.reshape(1, 4, 8, 8, NB)
    return run(step, parts, inverse, rhs.T).T


def solution(mesh):
    in_specs = (P(), P("row", "col"), P("row", "col"), P(None, "col"))
    out_specs = P("row", "col")
    return jax.shard_map(body, mesh=mesh, in_specs=in_specs, out_specs=out_specs, check_vma=False)
```

```python
import functools

import jax
import jax.numpy as jnp
from jax import lax
from jax.experimental import pallas as pl
from jax.experimental.pallas import tpu as pltpu
from jax.sharding import PartitionSpec as P

STEPS = 4
NB = 256
BLK = 6
MESH = pl.DeviceIdType.MESH
SPLIT = 640
WIDE = 1024
REST = WIDE - SPLIT
SEGMENTS = [
    [(True, 0, 0, 256)],
    [(True, 256, 0, 256)],
    [(True, 512, 0, 128), (False, 0, 128, 128)],
    [(False, 128, 0, 256)],
]
PAIRS = [(1, 0), (2, 0), (2, 1), (3, 0), (3, 1), (3, 2)]


def device(x, core, y, z):
    return (lax.rem(x + 8, 4) * 2 + core, lax.rem(y + 8, 4) * 8 + lax.rem(z + 16, 8))


def halve(value):
    high = value.astype(jnp.bfloat16)
    return high, (value - high.astype(jnp.float32)).astype(jnp.bfloat16)


def product(a, b):
    dot = functools.partial(
        lax.dot_general, dimension_numbers=(((1,), (1,)), ((), ())), preferred_element_type=jnp.float32)
    return dot(a[0], b[0]) + (dot(a[0], b[1]) + dot(a[1], b[0]))


def choose(index, values):
    result = values[0]
    for n, value in enumerate(values[1:], 1):
        result = jnp.where(index == n, value, result)
    return result


def step_kernel(step, factor, diag, rhs, acc, panels, r0, r1, r2, s0, s1, s2, p0, p1, p2, a1, b1, a2, b2, gathered,
                tc, tall, ycand, ypart, yhalf, ysel, solved, high, low, f_high, f_low, send, recv,
                local):
    start = step[0]
    row, col = lax.axis_index("row"), lax.axis_index("col")
    x, core = row // 2, lax.rem(row, 2)
    y, z = col // 8, lax.rem(col, 8)
    row_step = lax.rem(row - start + 32, 4)
    row_block = start + row_step
    row_local = row_block // 8
    row_real = lax.rem(row_block, 8) == row
    col_block = start + lax.rem(z - start + 32, 4)
    col_y = col_block // 8
    used = [0]
    sent = []

    def take(n=1):
        used[0] += n
        return used[0] - n

    def remote(src, dst, index, target):
        return pltpu.make_async_remote_copy(
            src_ref=src, dst_ref=dst, send_sem=send.at[index], recv_sem=recv.at[index],
            device_id=target, device_id_type=MESH)

    def push(src, dst, target):
        copy = remote(src, dst, take(), target)
        copy.start()
        sent.append(copy)
        return copy

    def arrived(copies):
        for copy in copies:
            copy.wait_recv()

    def at(dy=0, dz=0):
        return device(x, core, y + dy, z + dz)

    def across(dx=0, dc=0):
        return device(x + dx, lax.rem(core + dc, 2), y, z)

    barrier = pltpu.get_barrier_semaphore()
    others = [(dx, dc) for dx in range(4) for dc in (0, 1) if dx or dc]
    friends = [at(dy=d) for d in (1, -1, 2)] + [at(dz=d) for d in range(1, 8)] + [across(*o) for o in others]
    for friend in friends:
        pl.semaphore_signal(barrier, inc=1, device_id=friend, device_id_type=MESH)
    loads = [pltpu.make_async_copy(rhs.at[:, pl.ds(NB * l, NB)], acc.at[:, pl.ds(NB * l, NB)], local.at[l])
             for l in range(BLK)]
    fetches = [pltpu.make_async_copy(factor, panels, local.at[6]),
               pltpu.make_async_copy(diag, tc.at[pl.ds(0, 1)], local.at[7])]
    for load in fetches + loads:
        load.start()
    for fetch in fetches:
        fetch.wait()
    for ty in range(4):
        tc[1, ty] = choose(row_local, [panels[l, ty] for l in range(4)])
    pl.semaphore_wait(barrier, len(friends))

    class Scatter:
        def __init__(self, src, first, n, landing, stage, landed):
            self.src, self.first, self.n = src, first, n
            self.landing, self.stage, self.landed = landing, stage, landed

        def along_y(self):
            blocks = pl.ds(self.first, self.n)
            self.copies = [push(self.src.at[blocks, lax.rem(y + d + 4, 4)], self.landing.at[k], at(dy=d))
                           for k, d in enumerate((1, -1, 2))]

        def along_z(self):
            arrived(self.copies)
            back = lax.rem(y - col_y + 4, 4)
            for p in range(self.n):
                for tz in range(8):
                    self.stage[tz, p] = choose(back, [self.src[self.first + p, y, tz]] + [
                        self.landing[k, p, tz] for k in (0, 2, 1)])
            self.copies = [push(self.stage.at[lax.rem(z + d, 8)], self.landed.at[z], at(dz=d)) for d in range(1, 8)]
            self.landed[z] = self.stage[z]

        def arrive(self):
            arrived(self.copies)

        def pick(self, i, p):
            return choose(lax.rem(start + i, 8), [self.landed[n, p] for n in range(8)])

    class Chunk:
        def __init__(self, a, b, width, cut):
            self.a, self.b, self.width, self.cut = a, b, width, cut
            self.a_z, self.a_y, self.a_far, self.b_y, self.b_z = {}, {}, [], [], {}

        def move(self, ref, dy, dz):
            return push(ref, ref, at(dy=dy, dz=dz))

        def send_a_z(self, t):
            right, left = lax.rem(z - (t - 1) + 8, 8), lax.rem(z + (t - 1), 8)
            if t < 4:
                lanes = (pl.ds(0, self.width), pl.ds(0, self.width))
            else:
                lanes = (pl.ds(0, self.cut), pl.ds(self.cut, self.width - self.cut))
            self.a_z[t] = [self.move(self.a.at[y, right, :, :, lanes[0]], 0, 1),
                           self.move(self.a.at[y, left, :, :, lanes[1]], 0, -1)]

        def send_b_z(self, t):
            right, left = lax.rem(z - (t - 1) + 8, 8), lax.rem(z + (t - 1), 8)
            rows = (pl.ds(0, 4), pl.ds(0, 4)) if t < 4 else (pl.ds(0, 2), pl.ds(2, 2))
            self.b_z[t] = [self.move(self.b.at[right, rows[0]], 0, 1), self.move(self.b.at[left, rows[1]], 0, -1)]

        def send_a_y(self, t):
            origins = [lax.rem(z - t + 8, 8), lax.rem(z + t, 8)]
            if t in (0, 4):
                origins = origins[:1]
            self.a_y[t] = [self.move(self.a.at[y, o], d, 0) for o in origins for d in (1, -1)]

        def send_a_far(self, t):
            below, above = lax.rem(y + 3, 4), lax.rem(y + 1, 4)
            if t < 4:
                self.a_far.append(self.move(self.a.at[below, lax.rem(z - t + 8, 8)], 1, 0))
            if t > 0:
                self.a_far.append(self.move(self.a.at[above, lax.rem(z + t, 8)], -1, 0))

        def begin(self):
            self.send_a_z(1)
            if self.b is not None:
                self.b_y = [self.move(self.b.at[z, y], d, 0) for d in (1, -1, 2)]
            self.send_a_y(0)

        def step(self, t):
            if t <= 4:
                arrived(self.a_z[t])
                if t < 4:
                    self.send_a_z(t + 1)
                self.send_a_y(t)
            if self.b is not None:
                arrived(self.b_y if t == 1 else self.b_z[t - 1])
                if t <= 4:
                    self.send_b_z(t)
            arrived(self.a_y[t - 1])
            self.send_a_far(t - 1)

        def end(self):
            arrived(self.a_far)

    small = Scatter(tc, 0, 2, r0, s0, p0)
    first = Scatter(panels, 0, 3, r1, s1, p1)
    second = Scatter(panels, 3, 3, r2, s2, p2)
    g = Chunk(gathered.at[core], None, NB, 128)
    c1 = Chunk(a1, b1, SPLIT, 384)
    c2 = Chunk(a2, b2, SPLIT, 384)

    def place(scatter, a, b):
        for i in range(STEPS):
            for p in range(3):
                value = scatter.pick(i, p)
                for in_a, lane, source, n in SEGMENTS[i]:
                    part = value[:, source:source + n]
                    if in_a:
                        a[y, z, p, :, lane:lane + n] = part
                    else:
                        b[z, y, p, :, lane:lane + n] = part

    half = rhs.shape[0] // 2
    side = x // 2

    def candidates():
        for load in loads:
            load.wait()
        for h in (0, 1):
            ycand[h] = choose(row_local, [acc[pl.ds(half * h, half), pl.ds(NB * l, NB)] for l in range(4)])
        return push(ycand.at[1 - side], ypart, across(dx=2))

    def share(copy):
        arrived([copy])
        yhalf[...] = jnp.where(row_real, ycand[side], ypart[...])
        slot = lax.rem(row, 4)
        copies = [push(yhalf, ysel.at[slot, side], across(dx=d)) for d in (1, 3, 2)]
        copies.append(push(yhalf, ysel.at[slot, side], across(dc=1)))
        ysel[slot, side] = yhalf[...]
        return copies

    def relay(copies):
        arrived(copies[:3])
        passed = []
        for d in (1, 3, 2):
            sx = lax.rem(x - d + 4, 4)
            ref = ysel.at[lax.rem(2 * sx + core, 4), sx // 2]
            passed.append(push(ref, ref, across(dc=1)))
        return [copies[3]] + passed

    def triangle():
        for i in range(STEPS):
            tall[row, i] = small.pick(i, 1)
        return [push(tall.at[row], tall.at[row], across(*o)) for o in others]

    def payload():
        for m in range(2):
            gathered[core, y, z, m] = small.pick(2 * core + m, 0)
        for m in range(3):
            i = jnp.where(core == 0, PAIRS[m][0], PAIRS[3 + m][0])
            j = jnp.where(core == 0, PAIRS[m][1], PAIRS[3 + m][1])
            gathered[core, y, z, 2 + m] = choose(lax.rem(start + i, 8), [tall[n, j] for n in range(8)])

    def square(c, m):
        return halve(gathered[c, :, :, m].reshape(NB, NB))

    def solve(i):
        lanes = pl.ds(NB * i, NB)
        right = choose(lax.rem(start + i, 4), [ysel[n].reshape(2 * half, NB) for n in range(4)])
        for index, (k, j) in enumerate(PAIRS):
            if k == i:
                before = pl.ds(NB * j, NB)
                right = right - product((high[:, before], low[:, before]), square(index // 3, 2 + index % 3))
        value = product(halve(right), square(i // 2, i % 2))
        solved[...] = value if i == 0 else jnp.where(row_step == i, value, solved[...])
        high[:, lanes], low[:, lanes] = halve(value)

    def assemble(chunk, p, block):
        for ty in range(4):
            rows = pl.ds(64 * ty, 64)
            for i in range(STEPS):
                keep = start + i < block
                for in_a, lane, source, n in SEGMENTS[i]:
                    if in_a:
                        value = chunk.a[ty, :, p, :, lane:lane + n]
                    else:
                        value = chunk.b[:, ty, p, :, lane:lane + n]
                    value = jnp.where(keep, value.reshape(64, n), 0.0)
                    to = pl.ds(NB * i + source, n)
                    f_high[rows, to], f_low[rows, to] = halve(value)

    def update(chunk, p, l):
        assemble(chunk, p, l * 8 + row)
        lanes = pl.ds(NB * l, NB)
        value = acc[:, lanes] - product((high[...], low[...]), (f_high[...], f_low[...]))
        if l < 4:
            value = jnp.where(row_real & (row_local == l), solved[...], value)
        acc[:, lanes] = value

    small.along_y()
    first.along_y()
    second.along_y()
    small.along_z()
    ycopy = candidates()
    small.arrive()
    tcopies = triangle()
    first.along_z()
    arrived(tcopies)
    payload()
    g.begin()
    ycopies = share(ycopy)
    first.arrive()
    place(first, a1, b1)
    c1.begin()
    g.step(1)
    second.along_z()
    c1.step(1)
    g.step(2)
    second.arrive()
    place(second, a2, b2)
    c2.begin()
    g.step(3)
    c1.step(2)
    c2.step(1)
    g.step(4)
    c1.step(3)
    g.step(5)
    c2.step(2)
    g.end()
    gcopy = push(gathered.at[core], gathered.at[core], across(dc=1))
    c1.step(4)
    yrelays = relay(ycopies)
    c2.step(3)
    c1.step(5)
    arrived([gcopy] + yrelays)
    solve(0)
    solve(1)
    c2.step(4)
    solve(2)
    solve(3)
    c1.end()
    update(c1, 0, 0)
    c2.step(5)
    update(c1, 1, 1)
    update(c1, 2, 2)
    c2.end()
    update(c2,0,3)
    update(c2,1,4)
    update(c2,2,5)
    for copy in sent:
        copy.wait_send()
    assert used[0] <= send.shape[0], used[0]


def run(step, panels, diag, rhs):
    cols = rhs.shape[0]
    anywhere = pl.BlockSpec(memory_space=pl.ANY)
    inside = pl.BlockSpec(memory_space=pltpu.VMEM)
    f32, bf16 = jnp.float32, jnp.bfloat16
    shapes = [
        (BLK, 4, 8, 8, NB),
        (4, 2, 8, 8, NB), (4, 3, 8, 8, NB), (4, 3, 8, 8, NB),
        (8, 2, 8, NB), (8, 3, 8, NB), (8, 3, 8, NB),
        (8, 2, 8, NB), (8, 3, 8, NB), (8, 3, 8, NB),
        (4, 8, 3, 8, SPLIT), (8, 4, 3, 8, REST), (4, 8, 3, 8, SPLIT), (8, 4, 3, 8, REST),
        (2, 4, 8, 5, 8, NB),
        (2, 4, 8, 8, NB), (8, 4, 8, NB),
        (2, cols // 2, NB), (cols // 2, NB), (cols // 2, NB), (STEPS, 2, cols // 2, NB),
        (cols, NB),
    ]
    return pl.pallas_call(
        step_kernel,
        out_shape=pltpu.VMEM(rhs.shape, f32),
        in_specs=[pl.BlockSpec(memory_space=pltpu.SMEM), anywhere, anywhere, anywhere],
        out_specs=inside,
        scratch_shapes=[pltpu.VMEM(shape, f32) for shape in shapes] + [
            pltpu.VMEM((cols, WIDE), bf16),
            pltpu.VMEM((cols, WIDE), bf16),
            pltpu.VMEM((NB, WIDE), bf16),
            pltpu.VMEM((NB, WIDE), bf16),
            pltpu.SemaphoreType.DMA((224,)),
            pltpu.SemaphoreType.DMA((224,)),
            pltpu.SemaphoreType.DMA((16,)),
        ],
        compiler_params=pltpu.CompilerParams(
            collective_id=0, has_side_effects=True, vmem_limit_bytes=48 * 2**20),
        name="steps",
    )(step, panels, diag, rhs)


def body(step, rhs, panels, diag_inverses):
    parts = panels.reshape(BLK, 4, 8, 8, NB)
    inverse = diag_inverses.reshape(1, 4, 8, 8, NB)
    return run(step, parts, inverse, rhs.T).T


def solution(mesh):
    in_specs = (P(), P("row", "col"), P("row", "col"), P(None, "col"))
    out_specs = P("row", "col")
    return jax.shard_map(body, mesh=mesh, in_specs=in_specs, out_specs=out_specs, check_vma=False)
```

```python
import functools

import jax
import jax.numpy as jnp
from jax import lax
from jax.experimental import pallas as pl
from jax.experimental.pallas import tpu as pltpu
from jax.sharding import PartitionSpec as P

STEPS = 4
NB = 256
BLK = 6
MESH = pl.DeviceIdType.MESH
SPLIT = 640
WIDE = 1024
REST = WIDE - SPLIT
SEGMENTS = [
    [(True, 0, 0, 256)],
    [(True, 256, 0, 256)],
    [(True, 512, 0, 128), (False, 0, 128, 128)],
    [(False, 128, 0, 256)],
]
PAIRS = [(1, 0), (2, 0), (2, 1), (3, 0), (3, 1), (3, 2)]


def device(x, core, y, z):
    return (lax.rem(x + 8, 4) * 2 + core, lax.rem(y + 8, 4) * 8 + lax.rem(z + 16, 8))


def halve(value):
    high = value.astype(jnp.bfloat16)
    return high, (value - high.astype(jnp.float32)).astype(jnp.bfloat16)


def product(a, b):
    dot = functools.partial(
        lax.dot_general, dimension_numbers=(((1,), (1,)), ((), ())), preferred_element_type=jnp.float32)
    return dot(a[0], b[0]) + (dot(a[0], b[1]) + dot(a[1], b[0]))


def choose(index, values):
    result = values[0]
    for n, value in enumerate(values[1:], 1):
        result = jnp.where(index == n, value, result)
    return result


def step_kernel(step, factor, diag, rhs, acc, panels, r0, r1, r2, s0, s1, s2, p0, p1, p2, a1, b1, a2, b2, gathered,
                tc, tall, ycand, ypart, yhalf, ysel, solved, high, low, f_high, f_low, send, recv,
                local):
    start = step[0]
    row, col = lax.axis_index("row"), lax.axis_index("col")
    x, core = row // 2, lax.rem(row, 2)
    y, z = col // 8, lax.rem(col, 8)
    row_step = lax.rem(row - start + 32, 4)
    row_block = start + row_step
    row_local = row_block // 8
    row_real = lax.rem(row_block, 8) == row
    col_block = start + lax.rem(z - start + 32, 4)
    col_y = col_block // 8
    used = [0]
    sent = []

    def take(n=1):
        used[0] += n
        return used[0] - n

    def remote(src, dst, index, target):
        return pltpu.make_async_remote_copy(
            src_ref=src, dst_ref=dst, send_sem=send.at[index], recv_sem=recv.at[index],
            device_id=target, device_id_type=MESH)

    def push(src, dst, target):
        copy = remote(src, dst, take(), target)
        copy.start()
        sent.append(copy)
        return copy

    def arrived(copies):
        for copy in copies:
            copy.wait_recv()

    def at(dy=0, dz=0):
        return device(x, core, y + dy, z + dz)

    def across(dx=0, dc=0):
        return device(x + dx, lax.rem(core + dc, 2), y, z)

    barrier = pltpu.get_barrier_semaphore()
    others = [(dx, dc) for dx in range(4) for dc in (0, 1) if dx or dc]
    friends = [at(dy=d) for d in (1, -1, 2)] + [at(dz=d) for d in range(1, 8)] + [across(*o) for o in others]
    for friend in friends:
        pl.semaphore_signal(barrier, inc=1, device_id=friend, device_id_type=MESH)
    loads = [pltpu.make_async_copy(rhs.at[:, pl.ds(NB * l, NB)], acc.at[:, pl.ds(NB * l, NB)], local.at[l])
             for l in range(BLK)]
    fetches = [pltpu.make_async_copy(factor, panels, local.at[6]),
               pltpu.make_async_copy(diag, tc.at[pl.ds(0, 1)], local.at[7])]
    for load in fetches + loads:
        load.start()
    for fetch in fetches:
        fetch.wait()
    for ty in range(4):
        tc[1, ty] = choose(row_local, [panels[l, ty] for l in range(4)])
    pl.semaphore_wait(barrier, len(friends))

    class Scatter:
        def __init__(self, src, first, n, landing, stage, landed):
            self.src, self.first, self.n = src, first, n
            self.landing, self.stage, self.landed = landing, stage, landed

        def along_y(self):
            blocks = pl.ds(self.first, self.n)
            self.copies = [push(self.src.at[blocks, lax.rem(y + d + 4, 4)], self.landing.at[k], at(dy=d))
                           for k, d in enumerate((1, -1, 2))]

        def along_z(self):
            arrived(self.copies)
            back = lax.rem(y - col_y + 4, 4)
            for p in range(self.n):
                for tz in range(8):
                    self.stage[tz, p] = choose(back, [self.src[self.first + p, y, tz]] + [
                        self.landing[k, p, tz] for k in (0, 2, 1)])
            self.copies = [push(self.stage.at[lax.rem(z + d, 8)], self.landed.at[z], at(dz=d)) for d in range(1, 8)]
            self.landed[z] = self.stage[z]

        def arrive(self):
            arrived(self.copies)

        def pick(self, i, p):
            return choose(lax.rem(start + i, 8), [self.landed[n, p] for n in range(8)])

    class Chunk:
        def __init__(self, a, b, width, cut):
            self.a, self.b, self.width, self.cut = a, b, width, cut
            self.a_z, self.a_y, self.a_far, self.b_y, self.b_z = {}, {}, [], [], {}

        def move(self, ref, dy, dz):
            return push(ref, ref, at(dy=dy, dz=dz))

        def send_a_z(self, t):
            right, left = lax.rem(z - (t - 1) + 8, 8), lax.rem(z + (t - 1), 8)
            if t < 4:
                lanes = (pl.ds(0, self.width), pl.ds(0, self.width))
            else:
                lanes = (pl.ds(0, self.cut), pl.ds(self.cut, self.width - self.cut))
            self.a_z[t] = [self.move(self.a.at[y, right, :, :, lanes[0]], 0, 1),
                           self.move(self.a.at[y, left, :, :, lanes[1]], 0, -1)]

        def send_b_z(self, t):
            right, left = lax.rem(z - (t - 1) + 8, 8), lax.rem(z + (t - 1), 8)
            rows = (pl.ds(0, 4), pl.ds(0, 4)) if t < 4 else (pl.ds(0, 2), pl.ds(2, 2))
            self.b_z[t] = [self.move(self.b.at[right, rows[0]], 0, 1), self.move(self.b.at[left, rows[1]], 0, -1)]

        def send_a_y(self, t):
            origins = [lax.rem(z - t + 8, 8), lax.rem(z + t, 8)]
            if t in (0, 4):
                origins = origins[:1]
            self.a_y[t] = [self.move(self.a.at[y, o], d, 0) for o in origins for d in (1, -1)]

        def send_a_far(self, t):
            below, above = lax.rem(y + 3, 4), lax.rem(y + 1, 4)
            if t < 4:
                self.a_far.append(self.move(self.a.at[below, lax.rem(z - t + 8, 8)], 1, 0))
            if t > 0:
                self.a_far.append(self.move(self.a.at[above, lax.rem(z + t, 8)], -1, 0))

        def begin(self):
            self.send_a_z(1)
            if self.b is not None:
                self.b_y = [self.move(self.b.at[z, y], d, 0) for d in (1, -1, 2)]
            self.send_a_y(0)

        def step(self, t):
            if t <= 4:
                arrived(self.a_z[t])
                if t < 4:
                    self.send_a_z(t + 1)
                self.send_a_y(t)
            if self.b is not None:
                arrived(self.b_y if t == 1 else self.b_z[t - 1])
                if t <= 4:
                    self.send_b_z(t)
            arrived(self.a_y[t - 1])
            self.send_a_far(t - 1)

        def end(self):
            arrived(self.a_far)

    small = Scatter(tc, 0, 2, r0, s0, p0)
    first = Scatter(panels, 0, 4, r1, s1, p1)
    second = Scatter(panels, 4, 2, r2, s2, p2)
    g = Chunk(gathered.at[core], None, NB, 128)
    c1 = Chunk(a1, b1, SPLIT, 384)
    c2 = Chunk(a2, b2, SPLIT, 384)

    def place(scatter, a, b):
        for i in range(STEPS):
            for p in range(scatter.n):
                value = scatter.pick(i, p)
                for in_a, lane, source, n in SEGMENTS[i]:
                    part = value[:, source:source + n]
                    if in_a:
                        a[y, z, p, :, lane:lane + n] = part
                    else:
                        b[z, y, p, :, lane:lane + n] = part

    half = rhs.shape[0] // 2
    side = x // 2

    def candidates():
        for load in loads:
            load.wait()
        for h in (0, 1):
            ycand[h] = choose(row_local, [acc[pl.ds(half * h, half), pl.ds(NB * l, NB)] for l in range(4)])
        return push(ycand.at[1 - side], ypart, across(dx=2))

    def share(copy):
        arrived([copy])
        yhalf[...] = jnp.where(row_real, ycand[side], ypart[...])
        slot = lax.rem(row, 4)
        copies = [push(yhalf, ysel.at[slot, side], across(dx=d)) for d in (1, 3, 2)]
        copies.append(push(yhalf, ysel.at[slot, side], across(dc=1)))
        ysel[slot, side] = yhalf[...]
        return copies

    def relay(copies):
        arrived(copies[:3])
        passed = []
        for d in (1, 3, 2):
            sx = lax.rem(x - d + 4, 4)
            ref = ysel.at[lax.rem(2 * sx + core, 4), sx // 2]
            passed.append(push(ref, ref, across(dc=1)))
        return [copies[3]] + passed

    def triangle():
        for i in range(STEPS):
            tall[row, i] = small.pick(i, 1)
        return [push(tall.at[row], tall.at[row], across(*o)) for o in others]

    def payload():
        for m in range(2):
            gathered[core, y, z, m] = small.pick(2 * core + m, 0)
        for m in range(3):
            i = jnp.where(core == 0, PAIRS[m][0], PAIRS[3 + m][0])
            j = jnp.where(core == 0, PAIRS[m][1], PAIRS[3 + m][1])
            gathered[core, y, z, 2 + m] = choose(lax.rem(start + i, 8), [tall[n, j] for n in range(8)])

    def square(c, m):
        return halve(gathered[c, :, :, m].reshape(NB, NB))

    def solve(i):
        lanes = pl.ds(NB * i, NB)
        right = choose(lax.rem(start + i, 4), [ysel[n].reshape(2 * half, NB) for n in range(4)])
        for index, (k, j) in enumerate(PAIRS):
            if k == i:
                before = pl.ds(NB * j, NB)
                right = right - product((high[:, before], low[:, before]), square(index // 3, 2 + index % 3))
        value = product(halve(right), square(i // 2, i % 2))
        solved[...] = value if i == 0 else jnp.where(row_step == i, value, solved[...])
        high[:, lanes], low[:, lanes] = halve(value)

    def assemble(chunk, p, block):
        for ty in range(4):
            rows = pl.ds(64 * ty, 64)
            for i in range(STEPS):
                keep = start + i < block
                for in_a, lane, source, n in SEGMENTS[i]:
                    if in_a:
                        value = chunk.a[ty, :, p, :, lane:lane + n]
                    else:
                        value = chunk.b[:, ty, p, :, lane:lane + n]
                    value = jnp.where(keep, value.reshape(64, n), 0.0)
                    to = pl.ds(NB * i + source, n)
                    f_high[rows, to], f_low[rows, to] = halve(value)

    def update(chunk, p, l):
        assemble(chunk, p, l * 8 + row)
        lanes = pl.ds(NB * l, NB)
        value = acc[:, lanes] - product((high[...], low[...]), (f_high[...], f_low[...]))
        if l < 4:
            value = jnp.where(row_real & (row_local == l), solved[...], value)
        acc[:, lanes] = value

    small.along_y()
    first.along_y()
    second.along_y()
    small.along_z()
    ycopy = candidates()
    small.arrive()
    tcopies = triangle()
    first.along_z()
    arrived(tcopies)
    payload()
    g.begin()
    ycopies = share(ycopy)
    first.arrive()
    place(first, a1, b1)
    c1.begin()
    g.step(1)
    second.along_z()
    c1.step(1)
    g.step(2)
    second.arrive()
    place(second, a2, b2)
    c2.begin()
    g.step(3)
    c1.step(2)
    c2.step(1)
    g.step(4)
    c1.step(3)
    g.step(5)
    c2.step(2)
    g.end()
    gcopy = push(gathered.at[core], gathered.at[core], across(dc=1))
    c1.step(4)
    yrelays = relay(ycopies)
    c2.step(3)
    c1.step(5)
    arrived([gcopy] + yrelays)
    solve(0)
    solve(1)
    c2.step(4)
    solve(2)
    solve(3)
    c2.step(5)
    c1.end()
    update(c1, 0, 0)
    update(c1, 1, 1)
    update(c1, 2, 2)
    update(c1, 3, 3)
    c2.end()
    update(c2, 0, 4)
    update(c2, 1, 5)
    for copy in sent:
        copy.wait_send()
    assert used[0] <= send.shape[0], used[0]


def run(step, panels, diag, rhs):
    cols = rhs.shape[0]
    anywhere = pl.BlockSpec(memory_space=pl.ANY)
    inside = pl.BlockSpec(memory_space=pltpu.VMEM)
    f32, bf16 = jnp.float32, jnp.bfloat16
    shapes = [
        (BLK, 4, 8, 8, NB),
        (4, 2, 8, 8, NB), (4, 4, 8, 8, NB), (4, 2, 8, 8, NB),
        (8, 2, 8, NB), (8, 4, 8, NB), (8, 2, 8, NB),
        (8, 2, 8, NB), (8, 4, 8, NB), (8, 2, 8, NB),
        (4, 8, 4, 8, SPLIT), (8, 4, 4, 8, REST), (4, 8, 2, 8, SPLIT), (8, 4, 2, 8, REST),
        (2, 4, 8, 5, 8, NB),
        (2, 4, 8, 8, NB), (8, 4, 8, NB),
        (2, cols // 2, NB), (cols // 2, NB), (cols // 2, NB), (STEPS, 2, cols // 2, NB),
        (cols, NB),
    ]
    return pl.pallas_call(
        step_kernel,
        out_shape=pltpu.VMEM(rhs.shape, f32),
        in_specs=[pl.BlockSpec(memory_space=pltpu.SMEM), anywhere, anywhere, anywhere],
        out_specs=inside,
        scratch_shapes=[pltpu.VMEM(shape, f32) for shape in shapes] + [
            pltpu.VMEM((cols, WIDE), bf16),
            pltpu.VMEM((cols, WIDE), bf16),
            pltpu.VMEM((NB, WIDE), bf16),
            pltpu.VMEM((NB, WIDE), bf16),
            pltpu.SemaphoreType.DMA((224,)),
            pltpu.SemaphoreType.DMA((224,)),
            pltpu.SemaphoreType.DMA((16,)),
        ],
        compiler_params=pltpu.CompilerParams(
            collective_id=0, has_side_effects=True, vmem_limit_bytes=48 * 2**20),
        name="steps",
    )(step, panels, diag, rhs)


def body(step, rhs, panels, diag_inverses):
    parts = panels.reshape(BLK, 4, 8, 8, NB)
    inverse = diag_inverses.reshape(1, 4, 8, 8, NB)
    return run(step, parts, inverse, rhs.T).T


def solution(mesh):
    in_specs = (P(), P("row", "col"), P("row", "col"), P(None, "col"))
    out_specs = P("row", "col")
    return jax.shard_map(body, mesh=mesh, in_specs=in_specs, out_specs=out_specs, check_vma=False)
```
